256 devices in a mesh: dom: 64 (over y, z, core), rep: 4 (over x).
Axes of the slice: x: 4, y: 4, z: 8, core: 2. Of those that a mesh axis runs over, the one named last changes fastest.
Arguments:
- features: bfloat16 [131072, 256], P('dom', 'rep'), may hold values from -6 to 6
- order: int32 [64, 2048], P('dom'), may hold values from 0 to 2047, each once within a row
- weight: bfloat16 [256, 256], P('rep'), may hold values from -0.375 to 0.375
- bias: float32 [256], P('rep'), may hold values from -3 to 3
- tiles: bfloat16 [1024, 8, 128, 128], P('dom'), may hold values from -0.375 to 0.375
- col_ids: int32 [1024, 8], P('dom'), may hold values from 0 to 1023, as said below
- counts: int32 [1024], P('dom'), may hold values from 1 to 8, as said below
Outputs:
- activated: bfloat16 [131072, 256], P('dom', 'rep')
The draws below stay inside these ranges and needn't reach their ends.
Inputs may be any that keep to these rules, and one draw needn't show every extreme that they name: `col_ids`: block i belongs to index i // 16 of dom. Among the 128 slots of one index of dom, at most 2 name blocks of any one index, and some reach 2. `counts`: slots at or beyond the count are ignored. Every index of dom has a block row with 8.
All inputs are finite; a program needn't handle non-finite values.
Results may differ from the reference program's by a relative error of at most 0.0047.
Values may be sent and summed in bfloat16 or wider, within the bound.
No kernel may reach another device: no remote copies, remote signals or barrier semaphores. Data moves between devices by JAX's collectives and lax.ppermute only.
A program may use at most 128 MiB of HBM per device.

```python
import jax
import jax.numpy as jnp
from jax import lax

HID = 256
BLK = 128
MAXT = 8
RB = 16
DOMS = 64
CAP = 2
NODE_DEV = 2048
BLOCKS = 1024
NODES = 131072


def draw_col_ids(key, part):
    key = jax.random.fold_in(key, 11)

    def one_domain(index):
        own_key = jax.random.fold_in(key, index)
        first, second, third = jax.random.split(own_key, 3)
        holders = jax.random.permutation(first, DOMS)
        shuffled = jax.random.permutation(second, RB * MAXT)
        holder_ids = holders[shuffled // CAP]
        local_ids = jax.random.randint(third, (RB * MAXT,), 0, RB)
        return (holder_ids * RB + local_ids).astype(jnp.int32)
    every_domain = jax.vmap(one_domain)(jnp.arange(DOMS, dtype=jnp.int32))
    return every_domain.reshape(BLOCKS, MAXT)


def draw_counts(key, part):
    key = jax.random.fold_in(key, 23)
    first, second, third = jax.random.split(key, 3)
    levels = jax.random.randint(first, (DOMS, 1), 1, MAXT + 1)
    raw_counts = jax.random.randint(second, (DOMS, RB), 1, MAXT + 1)
    raw_counts = jnp.minimum(raw_counts, levels)
    full_rows = jax.random.randint(third, (DOMS, 1), 0, RB)
    positions = jnp.arange(RB, dtype=jnp.int32)[None, :]
    raw_counts = jnp.where(positions == full_rows, MAXT, raw_counts)
    return raw_counts.reshape(BLOCKS).astype(jnp.int32)


def shard_levels(key, shape, cuts, low, top_value):
    factor_of, own = 1.0, jax.random.fold_in(key, 6)
    for position, shards_of in cuts:
        draws = jnp.exp(jax.random.uniform(jax.random.fold_in(own, position), (shards_of,), jnp.float32, low / len(cuts), top_value / len(cuts)))
        factor_of = factor_of * jnp.repeat(draws, shape[position] // shards_of).reshape([-1 if axis == position else 1 for axis in range(len(shape))])
    return factor_of


def normal_values(rng, shape, scale, most, cuts=(), kind=jnp.bfloat16):
    factor_of = shard_levels(rng, shape, cuts, -0.22, 0.18) if cuts else 1.0
    drawn = jax.random.normal(rng, shape, jnp.float32) * scale * factor_of
    return jnp.minimum(jnp.maximum(drawn, -most), most).astype(kind)


def setup_inputs(seed: int = 0) -> dict:
    arg_keys = jax.random.split(jax.random.key(seed), 8)
    return {
        "features": normal_values(arg_keys[0], (NODES, HID), 1.0, 6.0, ((0, 64), (1, 4))),
        "order": jax.vmap(lambda own: jax.random.permutation(own, NODE_DEV))(jax.random.split(arg_keys[1], DOMS)).reshape((DOMS, NODE_DEV)).astype(jnp.int32),
        "weight": normal_values(arg_keys[2], (HID, HID), HID ** -0.5, 0.375, ((0, 4),)),
        "bias": normal_values(arg_keys[3], (HID,), 0.5, 3.0, ((0, 4),), jnp.float32),
        "tiles": normal_values(arg_keys[4], (BLOCKS, MAXT, BLK, BLK), (BLK * MAXT // 4) ** -0.5, 0.375, ((0, 64),)),
        "col_ids": draw_col_ids(jax.random.fold_in(arg_keys[7], 71), 0),
        "counts": draw_counts(jax.random.fold_in(arg_keys[7], 71), 0),
    }


def reference(features, order, weight, bias, tiles, col_ids, counts):
    grouped = features.reshape(DOMS, NODE_DEV, HID)
    reordered = jnp.take_along_axis(grouped, order[:, :, None], axis=1).reshape(NODES, HID)
    hidden = jnp.dot(reordered, weight, preferred_element_type=jnp.float32).astype(jnp.bfloat16)
    node_blocks = hidden.reshape(BLOCKS, BLK, HID)
    slot_index = jnp.arange(MAXT, dtype=jnp.int32)

    def one_row(inputs):
        tile_row, id_row, count_row = inputs
        used_mask = (slot_index < count_row).astype(jnp.float32)
        fetched = node_blocks[id_row].astype(jnp.float32) * used_mask[:, None, None]
        return jnp.einsum("kij,kjf->if", tile_row.astype(jnp.float32), fetched)

    summed = lax.map(one_row, (tiles, col_ids, counts))
    activated = jax.nn.relu(summed.reshape(NODES, HID) + bias[None, :])
    return activated.astype(jnp.bfloat16)
```

```python
import jax
import jax.numpy as jnp
from jax import lax
from jax.experimental import pallas as pl
from jax.experimental.pallas import tpu as pltpu
from jax.sharding import PartitionSpec as P

VMEM_LIMIT = 48 * 1024 * 1024


def send_kernel(req_ref, rep_ref, order_ref, x0_ref, x1_ref, x2_ref, x3_ref, send_ref, blocks):
    width = x0_ref.shape[0]
    nodes = order_ref.shape[1]
    count = blocks.shape[0]
    size = blocks.shape[2]
    rep = rep_ref[0]
    total = jnp.zeros((width, nodes), jnp.float32)
    for part in (x0_ref, x1_ref, x2_ref, x3_ref):
        columns = part[:, nodes : nodes + width]
        for index in range(1, (part.shape[1] - nodes) // width):
            other = part[:, nodes + index * width : nodes + (index + 1) * width]
            columns = jnp.where(rep == index, other, columns)
        total += lax.dot_general(
            columns,
            part[:, :nodes],
            (((0,), (0,)), ((), ())),
            preferred_element_type=jnp.float32,
        )
    hidden = total.astype(jnp.bfloat16).astype(jnp.float32)
    for block in range(count):
        order = order_ref[:, block * size : (block + 1) * size]
        order = jnp.broadcast_to(order, (width, size))
        lane = jnp.bitwise_and(order, size - 1)
        chunk = lax.shift_right_logical(order, size.bit_length() - 1)
        value = jnp.zeros((width, size), jnp.float32)
        for source in range(count):
            piece = hidden[:, source * size : (source + 1) * size]
            picked = jnp.take_along_axis(piece, lane, axis=1)
            value = jnp.where(chunk == source, picked, value)
        blocks[block] = value.astype(jnp.bfloat16)

    def copy(target, carry):
        for slot in range(2):
            wanted = jnp.bitwise_and(req_ref[target, slot * 64], count - 1)
            send_ref[target, slot] = blocks[wanted]
        return carry

    lax.fori_loop(0, send_ref.shape[0], copy, 0, unroll=8)


def make_send(req, rep, order, parts, width, nodes, size, owners):
    return pl.pallas_call(
        send_kernel,
        out_shape=jax.ShapeDtypeStruct((owners, 2, width, size), jnp.bfloat16),
        in_specs=[pl.BlockSpec(memory_space=pltpu.SMEM)] * 2
        + [pl.BlockSpec(memory_space=pltpu.VMEM)] * (1 + len(parts)),
        out_specs=pl.BlockSpec(memory_space=pltpu.VMEM),
        scratch_shapes=[pltpu.VMEM((nodes // size, width, size), jnp.bfloat16)],
        compiler_params=pltpu.CompilerParams(vmem_limit_bytes=VMEM_LIMIT),
        name="send_blocks",
    )(req, rep, order, *parts)


def sum_kernel(place_ref, counts_ref, tiles_ref, bias_ref, got_ref, out_ref):
    row = pl.program_id(0)
    slots = tiles_ref.shape[1]
    used = counts_ref[row]
    pieces = []
    for slot in range(slots):
        piece = got_ref[place_ref[row * slots + slot]]
        pieces.append(jnp.where(slot < used, piece, jnp.zeros_like(piece)))
    gathered = jnp.concatenate(pieces, axis=1)
    tiles = jnp.concatenate([tiles_ref[0, slot] for slot in range(slots)], axis=1)
    summed = lax.dot_general(
        gathered, tiles, (((1,), (1,)), ((), ())), preferred_element_type=jnp.float32
    )
    out_ref[...] = jnp.maximum(summed + bias_ref[...], 0.0).astype(out_ref.dtype)


def make_sum(place, counts, tiles, bias, got):
    rows, slots, size, _ = tiles.shape
    width = bias.shape[0]
    return pl.pallas_call(
        sum_kernel,
        grid_spec=pltpu.PrefetchScalarGridSpec(
            num_scalar_prefetch=2,
            grid=(rows,),
            in_specs=[
                pl.BlockSpec((1, slots, size, size), lambda row, *_: (row, 0, 0, 0)),
                pl.BlockSpec((width, 1), lambda row, *_: (0, 0)),
                pl.BlockSpec(got.shape, lambda row, *_: (0, 0, 0)),
            ],
            out_specs=pl.BlockSpec((width, size), lambda row, *_: (0, row)),
        ),
        out_shape=jax.ShapeDtypeStruct((width, rows * size), jnp.bfloat16),
        compiler_params=pltpu.CompilerParams(vmem_limit_bytes=VMEM_LIMIT),
        name="sum_tiles",
    )(place, counts, tiles, bias, got)


def body(features, order, weight, bias, tiles, col_ids, counts):
    nodes, width = features.shape
    rows, slots, size, _ = tiles.shape
    owners = lax.axis_size("dom")
    reps = lax.axis_size("rep")
    rep = lax.axis_index("rep").astype(jnp.int32)
    mine = jnp.concatenate([features.T, weight], axis=1)
    parts = [mine] + [
        lax.ppermute(mine, "rep", [(i, (i + shift) % reps) for i in range(reps)])
        for shift in range(1, reps)
    ]
    ids = col_ids.reshape(-1)
    total = ids.shape[0]
    owner = ids // rows
    slot = jnp.arange(total, dtype=jnp.int32)
    code = slot * rows + ids % rows
    match = owner[None, :] == jnp.arange(owners, dtype=jnp.int32)[:, None]
    first = jnp.min(jnp.where(match, code[None, :], total * rows), axis=1)
    last = jnp.max(jnp.where(match, code[None, :], -1), axis=1)
    request = jnp.concatenate(
        [jnp.broadcast_to(v[:, None], (owners, 64)) for v in (first, last)], axis=1
    )
    request = lax.all_to_all(request % rows, "dom", 0, 0, tiled=True)
    earlier = (owner[None, :] == owner[:, None]) & (slot[None, :] < slot[:, None])
    place = owner * 2 + jnp.any(earlier, axis=1).astype(jnp.int32)
    send = make_send(request, rep[None], order, parts, width, nodes, size, owners)
    got = lax.all_to_all(send.reshape(owners, 2 * width, size), "dom", 0, 0, tiled=True)
    out = make_sum(place, counts, tiles, bias[:, None], got.reshape(owners * 2, width, size))
    return out.T


def solution(mesh):
    in_specs = (
        P("dom", "rep"),
        P("dom", None),
        P("rep", None),
        P("rep"),
        P("dom", None, None, None),
        P("dom", None),
        P("dom"),
    )
    out_specs = P("dom", "rep")
    return jax.shard_map(body, mesh=mesh, in_specs=in_specs, out_specs=out_specs, check_vma=False)
```

```python
import jax
import jax.numpy as jnp
from jax import lax
from jax.experimental import pallas as pl
from jax.experimental.pallas import tpu as pltpu
from jax.sharding import PartitionSpec as P

VMEM_LIMIT = 40 * 1024 * 1024
VMEM = pl.BlockSpec(memory_space=pltpu.VMEM)
SMEM = pl.BlockSpec(memory_space=pltpu.SMEM)


def hidden_kernel(rep_ref, order_ref, x0_ref, x1_ref, x2_ref, x3_ref, blocks_ref):
    width = x0_ref.shape[0]
    count, _, size = blocks_ref.shape
    nodes = count * size
    rep = rep_ref[0]
    weights = []
    features = []
    for part in (x0_ref, x1_ref, x2_ref, x3_ref):
        columns = part[:, nodes : nodes + width]
        for index in range(1, (part.shape[1] - nodes) // width):
            other = part[:, nodes + index * width : nodes + (index + 1) * width]
            columns = jnp.where(rep == index, other, columns)
        weights.append(columns)
        features.append(part[:, :nodes])
    total = lax.dot_general(
        jnp.concatenate(weights, axis=0),
        jnp.concatenate(features, axis=0),
        (((0,), (0,)), ((), ())),
        preferred_element_type=jnp.float32,
    )
    hidden = total.astype(jnp.bfloat16).astype(jnp.float32)
    for block in range(count):
        order = order_ref[:, block * size : (block + 1) * size]
        order = jnp.broadcast_to(order, (width, size))
        lane = jnp.bitwise_and(order, size - 1)
        chunk = lax.shift_right_logical(order, size.bit_length() - 1)
        value = jnp.zeros((width, size), jnp.float32)
        for source in range(count):
            piece = hidden[:, source * size : (source + 1) * size]
            picked = jnp.take_along_axis(piece, lane, axis=1)
            value = jnp.where(chunk == source, picked, value)
        blocks_ref[block] = value.astype(jnp.bfloat16)


def make_hidden(rep, order, parts, width, nodes, size):
    return pl.pallas_call(
        hidden_kernel,
        out_shape=jax.ShapeDtypeStruct((nodes // size, width, size), jnp.bfloat16),
        in_specs=[SMEM] + [VMEM] * (1 + len(parts)),
        out_specs=VMEM,
        compiler_params=pltpu.CompilerParams(vmem_limit_bytes=VMEM_LIMIT),
        cost_estimate=pl.CostEstimate(flops=400_000_000, bytes_accessed=8_000_000, transcendentals=0),
        name="hidden_blocks",
    )(rep, order, *parts)


def pick_kernel(req_ref, blocks_ref, send_ref):
    count = blocks_ref.shape[0]

    def copy(target, carry):
        for slot in range(2):
            wanted = jnp.bitwise_and(req_ref[target, slot * 64], count - 1)
            send_ref[target, slot] = blocks_ref[wanted]
        return carry

    lax.fori_loop(0, send_ref.shape[0], copy, 0, unroll=8)


def make_pick(req, blocks):
    owners = req.shape[0]
    return pl.pallas_call(
        pick_kernel,
        out_shape=jax.ShapeDtypeStruct((owners, 2) + blocks.shape[1:], jnp.bfloat16),
        in_specs=[SMEM, VMEM],
        out_specs=VMEM,
        compiler_params=pltpu.CompilerParams(vmem_limit_bytes=VMEM_LIMIT),
        name="pick_blocks",
    )(req, blocks)


def sum_kernel(place_ref, counts_ref, tiles_ref, bias_ref, got_ref, out_ref):
    rows, slots, size, _ = tiles_ref.shape
    for row in range(rows):
        used = counts_ref[row]
        pieces = []
        for slot in range(slots):
            piece = got_ref[place_ref[row * slots + slot]]
            pieces.append(jnp.where(slot < used, piece, jnp.zeros_like(piece)))
        gathered = jnp.concatenate(pieces, axis=1)
        tiles = jnp.concatenate([tiles_ref[row, slot] for slot in range(slots)], axis=1)
        summed = lax.dot_general(
            gathered, tiles, (((1,), (1,)), ((), ())), preferred_element_type=jnp.float32
        )
        out_ref[:, row * size : (row + 1) * size] = jnp.maximum(
            summed + bias_ref[...], 0.0
        ).astype(out_ref.dtype)


def make_sum(place, counts, tiles, bias, got):
    rows, _, size, _ = tiles.shape
    return pl.pallas_call(
        sum_kernel,
        out_shape=jax.ShapeDtypeStruct((bias.shape[0], rows * size), jnp.bfloat16),
        in_specs=[SMEM, SMEM, VMEM, VMEM, VMEM],
        out_specs=VMEM,
        compiler_params=pltpu.CompilerParams(vmem_limit_bytes=VMEM_LIMIT),
        name="sum_tiles",
    )(place, counts, tiles, bias, got)


def body(features, order, weight, bias, tiles, col_ids, counts):
    nodes, width = features.shape
    rows, slots, size, _ = tiles.shape
    owners = lax.axis_size("dom")
    reps = lax.axis_size("rep")
    rep = lax.axis_index("rep").astype(jnp.int32)
    mine = jnp.concatenate([features.T, weight], axis=1)
    parts = [mine] + [
        lax.ppermute(mine, "rep", [(i, (i + shift) % reps) for i in range(reps)])
        for shift in range(1, reps)
    ]
    ids = col_ids.reshape(-1)
    total = ids.shape[0]
    owner = ids // rows
    slot = jnp.arange(total, dtype=jnp.int32)
    code = slot * rows + ids % rows
    match = owner[None, :] == jnp.arange(owners, dtype=jnp.int32)[:, None]
    first = jnp.min(jnp.where(match, code[None, :], total * rows), axis=1)
    last = jnp.max(jnp.where(match, code[None, :], -1), axis=1)
    request = jnp.concatenate(
        [jnp.broadcast_to(v[:, None], (owners, 64)) for v in (first, last)], axis=1
    )
    request = lax.all_to_all(request % rows, "dom", 0, 0, tiled=True)
    earlier = (owner[None, :] == owner[:, None]) & (slot[None, :] < slot[:, None])
    place = owner * 2 + jnp.any(earlier, axis=1).astype(jnp.int32)
    blocks = make_hidden(rep[None], order, parts, width, nodes, size)
    send = make_pick(request, blocks)
    got = lax.all_to_all(send.reshape(owners, 2 * width, size), "dom", 0, 0, tiled=True)
    out = make_sum(place, counts, tiles, bias[:, None], got.reshape(owners * 2, width, size))
    return out.T


def solution(mesh):
    in_specs = (
        P("dom", "rep"),
        P("dom", None),
        P("rep", None),
        P("rep"),
        P("dom", None, None, None),
        P("dom", None),
        P("dom"),
    )
    out_specs = P("dom", "rep")
    return jax.shard_map(body, mesh=mesh, in_specs=in_specs, out_specs=out_specs, check_vma=False)
```

```python
import functools

import jax
import jax.numpy as jnp
from jax import lax
from jax.experimental import pallas as pl
from jax.experimental.pallas import tpu as pltpu
from jax.sharding import PartitionSpec as P

VMEM_LIMIT = 24 * 1024 * 1024
VMEM = pl.BlockSpec(memory_space=pltpu.VMEM)
SMEM = pl.BlockSpec(memory_space=pltpu.SMEM)
Y, Z, CORES = 4, 8, 2
CHUNKS = ((0, -1, 1), (-2, 2), (-3, 3), (4,))


def hidden_kernel(rep_ref, order_ref, x0_ref, x1_ref, x2_ref, x3_ref, blocks_ref):
    width = x0_ref.shape[0]
    count, _, size = blocks_ref.shape
    nodes = count * size
    rep = rep_ref[0]
    weights = []
    features = []
    for part in (x0_ref, x1_ref, x2_ref, x3_ref):
        columns = part[:, nodes : nodes + width]
        for index in range(1, (part.shape[1] - nodes) // width):
            other = part[:, nodes + index * width : nodes + (index + 1) * width]
            columns = jnp.where(rep == index, other, columns)
        weights.append(columns)
        features.append(part[:, :nodes])
    total = lax.dot_general(
        jnp.concatenate(weights, axis=0),
        jnp.concatenate(features, axis=0),
        (((0,), (0,)), ((), ())),
        preferred_element_type=jnp.float32,
    )
    hidden = total.astype(jnp.bfloat16).astype(jnp.float32)
    for block in range(count):
        order = order_ref[:, block * size : (block + 1) * size]
        order = jnp.broadcast_to(order, (width, size))
        lane = jnp.bitwise_and(order, size - 1)
        chunk = lax.shift_right_logical(order, size.bit_length() - 1)
        value = jnp.zeros((width, size), jnp.float32)
        for source in range(count):
            piece = hidden[:, source * size : (source + 1) * size]
            picked = jnp.take_along_axis(piece, lane, axis=1)
            value = jnp.where(chunk == source, picked, value)
        blocks_ref[block] = value.astype(jnp.bfloat16)


def make_hidden(rep, order, parts, width, nodes, size):
    return pl.pallas_call(
        hidden_kernel,
        out_shape=jax.ShapeDtypeStruct((nodes // size, width, size), jnp.bfloat16),
        in_specs=[SMEM] + [VMEM] * (1 + len(parts)),
        out_specs=VMEM,
        compiler_params=pltpu.CompilerParams(vmem_limit_bytes=VMEM_LIMIT),
        cost_estimate=pl.CostEstimate(flops=400_000_000, bytes_accessed=8_000_000, transcendentals=0),
        name="hidden_blocks",
    )(rep, order, *parts)


def pick_kernel(near, count, request_ref, place_ref, *refs):
    own_ref, core_ref, *send_refs = refs[-(1 + Y) :]
    sources = refs[: -(1 + Y)]
    y, z, core = place_ref[0], place_ref[1], place_ref[2]
    half = count // 2

    def block(index, wanted):
        if index < len(near) - 1 or near[index] != Z // 2:
            return sources[index][wanted]
        low = sources[index][jnp.minimum(wanted, half - 1)]
        high = sources[index + 1][jnp.maximum(wanted - half, 0)]
        return jnp.where(wanted < half, low, high)

    for shift in range(Y):
        for other in range(CORES):
            row = lax.rem(y + shift, Y) * CORES + jnp.bitwise_xor(core, other)
            for index, offset in enumerate(near):
                owner = lax.rem(z + offset + Z, Z)
                for slot in range(2):
                    wanted = jnp.bitwise_and(request_ref[row, owner * 2 + slot], count - 1)
                    value = block(index, wanted)
                    if shift:
                        send_refs[shift - 1][other, index, slot] = value
                    elif other:
                        core_ref[index, slot] = value
                    else:
                        own_ref[index, slot] = value


def make_pick(near, count, request, place, sources):
    piece = sources[0].shape[1:]
    one = jax.ShapeDtypeStruct((len(near), 2) + piece, jnp.bfloat16)
    both = jax.ShapeDtypeStruct((CORES, len(near), 2) + piece, jnp.bfloat16)
    return pl.pallas_call(
        functools.partial(pick_kernel, near, count),
        out_shape=(one, one) + (both,) * (Y - 1),
        in_specs=[SMEM, SMEM] + [VMEM] * len(sources),
        out_specs=(VMEM,) * (1 + Y),
        compiler_params=pltpu.CompilerParams(vmem_limit_bytes=VMEM_LIMIT),
        name="pick_blocks",
    )(request, place, *sources)


def sum_kernel(where_ref, tiles_ref, bias_ref, *refs):
    *parts, out_ref, got_ref = refs
    start = 0
    for chunk in range(0, len(parts), Y + 1):
        own_ref, *arrived, swapped_ref = parts[chunk : chunk + Y + 1]
        pairs = own_ref.shape[0]
        for shift in range(Y):
            for other in range(CORES):
                base = (shift * CORES + other) * Z * 2 + start
                for pair in range(pairs):
                    for slot in range(2):
                        if other:
                            value = swapped_ref[shift, pair, slot]
                        elif shift:
                            value = arrived[shift - 1][0, pair, slot]
                        else:
                            value = own_ref[pair, slot]
                        got_ref[base + pair * 2 + slot] = value
        start += pairs * 2
    rows, slots, size, _ = tiles_ref.shape
    for row in range(rows):
        pieces = [got_ref[where_ref[row * slots + slot]] for slot in range(slots)]
        gathered = jnp.concatenate(pieces, axis=1)
        tiles = jnp.concatenate([tiles_ref[row, slot] for slot in range(slots)], axis=1)
        summed = lax.dot_general(
            gathered, tiles, (((1,), (1,)), ((), ())), preferred_element_type=jnp.float32
        )
        out_ref[:, row * size : (row + 1) * size] = jnp.maximum(
            summed + bias_ref[...], 0.0
        ).astype(out_ref.dtype)


def make_sum(where, tiles, bias, parts):
    rows, slots, size, _ = tiles.shape
    width = bias.shape[0]
    return pl.pallas_call(
        sum_kernel,
        out_shape=jax.ShapeDtypeStruct((width, rows * size), jnp.bfloat16),
        in_specs=[SMEM, VMEM, VMEM] + [VMEM] * len(parts),
        out_specs=VMEM,
        scratch_shapes=[pltpu.VMEM((rows * slots, width, size), jnp.bfloat16)],
        compiler_params=pltpu.CompilerParams(vmem_limit_bytes=VMEM_LIMIT),
        name="sum_tiles",
    )(where, tiles, bias, *parts)


def load_kernel(counts_ref, tiles_ref, used_ref):
    rows, slots = tiles_ref.shape[:2]

    def load(row, carry):
        for slot in range(slots):
            tile = tiles_ref[row, slot]
            used_ref[row, slot] = jnp.where(slot < counts_ref[row], tile, jnp.zeros_like(tile))
        return carry

    lax.fori_loop(0, rows, load, 0, unroll=2)


def make_load(counts, tiles):
    return pl.pallas_call(
        load_kernel,
        out_shape=jax.ShapeDtypeStruct(tiles.shape, tiles.dtype),
        in_specs=[SMEM, VMEM],
        out_specs=VMEM,
        compiler_params=pltpu.CompilerParams(vmem_limit_bytes=VMEM_LIMIT),
        cost_estimate=pl.CostEstimate(flops=0, bytes_accessed=8_000_000, transcendentals=0),
        name="load_tiles",
    )(counts, tiles)


def dom_index(y, z, core):
    return (y * Z + z) * CORES + core


def move(array, shift_y, shift_z, other):
    pairs = [
        (
            dom_index(y, z, core),
            dom_index((y + shift_y) % Y, (z + shift_z) % Z, core ^ other),
        )
        for y in range(Y)
        for z in range(Z)
        for core in range(CORES)
    ]
    return lax.ppermute(array, "dom", pairs)


def body(features, order, weight, bias, tiles, col_ids, counts):
    nodes, width = features.shape
    rows, slots, size, _ = tiles.shape
    reps = lax.axis_size("rep")
    rep = lax.axis_index("rep").astype(jnp.int32)
    dom = lax.axis_index("dom").astype(jnp.int32)
    y, z, core = dom // (Z * CORES), (dom // CORES) % Z, dom % CORES
    mine = jnp.concatenate([features.T, weight], axis=1)
    parts = [mine] + [
        lax.ppermute(mine, "rep", [(i, (i + shift) % reps) for i in range(reps)])
        for shift in range(1, reps)
    ]

    ids = col_ids.reshape(-1)
    total = ids.shape[0]
    owner = ids // rows
    slot = jnp.arange(total, dtype=jnp.int32)
    code = slot * rows + ids % rows
    row = lax.broadcasted_iota(jnp.int32, (Y * CORES, 128), 0)
    lane = lax.broadcasted_iota(jnp.int32, (Y * CORES, 128), 1)
    asked = dom_index(row // CORES, (lane // 2) % Z, row % CORES)
    match = owner[None, None, :] == asked[:, :, None]
    first = jnp.min(jnp.where(match, code[None, None, :], total * rows), axis=2)
    last = jnp.max(jnp.where(match, code[None, None, :], -1), axis=2)
    request = jnp.where(lane % 2 == 0, first, last) % rows
    groups = [
        [dom_index(group_y, group_z, group_core) for group_y in range(Y) for group_core in range(CORES)]
        for group_z in range(Z)
    ]
    request = lax.all_to_all(request, "dom", 0, 0, axis_index_groups=groups, tiled=True)

    earlier = (owner[None, :] == owner[:, None]) & (slot[None, :] < slot[:, None])
    rank = jnp.any(earlier, axis=1).astype(jnp.int32)
    away = ((owner // CORES) % Z - z) % Z
    found = jnp.zeros_like(away)
    for index, offset in enumerate(sum(CHUNKS, ())):
        found = jnp.where(away == offset % Z, index, found)
    shift = (y - owner // (Z * CORES)) % Y
    other = jnp.bitwise_xor(owner % CORES, core)
    where = ((shift * CORES + other) * Z + found) * 2 + rank

    used = make_load(counts, tiles)
    request, used, *parts = lax.optimization_barrier((request, used, *parts))
    blocks = make_hidden(rep[None], order, parts, width, nodes, size)
    ups, downs = [blocks], [blocks]
    for _ in range(Z // 2 - 1):
        ups.append(move(ups[-1], 0, 1, 0))
        downs.append(move(downs[-1], 0, -1, 0))
    half = rows // 2
    opposite = [move(ups[-1][:half], 0, 1, 0), move(downs[-1][half:], 0, -1, 0)]
    held = {0: [blocks], -Z // 2: opposite}
    for step in range(1, Z // 2):
        held[-step] = [ups[step]]
        held[step] = [downs[step]]
    held[Z // 2] = opposite

    place = jnp.stack([y, z, core])
    got = []
    for near in CHUNKS:
        sources = [array for offset in near for array in held[offset]]
        own, swap, *sends = make_pick(near, rows, request, place, sources)
        arrived = [move(send, step + 1, 0, 0) for step, send in enumerate(sends)]
        swap = jnp.stack([swap] + [array[1] for array in arrived])
        got += [own] + arrived + [move(swap, 0, 0, 1)]
    return make_sum(where, used, bias[:, None], got).T


def solution(mesh):
    in_specs = (
        P("dom", "rep"),
        P("dom", None),
        P("rep", None),
        P("rep"),
        P("dom", None, None, None),
        P("dom", None),
        P("dom"),
    )
    out_specs = P("dom", "rep")
    return jax.shard_map(body, mesh=mesh, in_specs=in_specs, out_specs=out_specs, check_vma=False)
```

```python
import functools

import jax
import jax.numpy as jnp
from jax import lax
from jax.experimental import pallas as pl
from jax.experimental.pallas import tpu as pltpu
from jax.sharding import PartitionSpec as P

VMEM_LIMIT = 24 * 1024 * 1024
VMEM = pl.BlockSpec(memory_space=pltpu.VMEM)
SMEM = pl.BlockSpec(memory_space=pltpu.SMEM)
Y, Z, CORES = 4, 8, 2
CHUNKS = ((0, -1), (1, -2, 2), (-3, 3), (4,))


def hidden_kernel(rep_ref, order_ref, x0_ref, x1_ref, x2_ref, x3_ref, blocks_ref):
    width = x0_ref.shape[0]
    count, _, size = blocks_ref.shape
    nodes = count * size
    rep = rep_ref[0]
    weights = []
    features = []
    for part in (x0_ref, x1_ref, x2_ref, x3_ref):
        columns = part[:, nodes : nodes + width]
        for index in range(1, (part.shape[1] - nodes) // width):
            other = part[:, nodes + index * width : nodes + (index + 1) * width]
            columns = jnp.where(rep == index, other, columns)
        weights.append(columns)
        features.append(part[:, :nodes])
    total = lax.dot_general(
        jnp.concatenate(weights, axis=0),
        jnp.concatenate(features, axis=0),
        (((0,), (0,)), ((), ())),
        preferred_element_type=jnp.float32,
    )
    hidden = total.astype(jnp.bfloat16).astype(jnp.float32)
    for block in range(count):
        order = order_ref[:, block * size : (block + 1) * size]
        order = jnp.broadcast_to(order, (width, size))
        lane = jnp.bitwise_and(order, size - 1)
        chunk = lax.shift_right_logical(order, size.bit_length() - 1)
        value = jnp.zeros((width, size), jnp.float32)
        for source in range(count):
            piece = hidden[:, source * size : (source + 1) * size]
            picked = jnp.take_along_axis(piece, lane, axis=1)
            value = jnp.where(chunk == source, picked, value)
        blocks_ref[block] = value.astype(jnp.bfloat16)


def make_hidden(rep, order, parts, width, nodes, size):
    return pl.pallas_call(
        hidden_kernel,
        out_shape=jax.ShapeDtypeStruct((nodes // size, width, size), jnp.bfloat16),
        in_specs=[SMEM] + [VMEM] * (1 + len(parts)),
        out_specs=VMEM,
        compiler_params=pltpu.CompilerParams(vmem_limit_bytes=VMEM_LIMIT),
        cost_estimate=pl.CostEstimate(flops=400_000_000, bytes_accessed=8_000_000, transcendentals=0),
        name="hidden_blocks",
    )(rep, order, *parts)


def pick_kernel(near, count, request_ref, place_ref, *refs):
    own_ref, core_ref, *send_refs = refs[-(1 + Y) :]
    sources = refs[: -(1 + Y)]
    y, z, core = place_ref[0], place_ref[1], place_ref[2]
    half = count // 2

    def block(index, wanted):
        if index < len(near) - 1 or near[index] != Z // 2:
            return sources[index][wanted]
        low = sources[index][jnp.minimum(wanted, half - 1)]
        high = sources[index + 1][jnp.maximum(wanted - half, 0)]
        return jnp.where(wanted < half, low, high)

    for shift in range(Y):
        for other in range(CORES):
            row = lax.rem(y + shift, Y) * CORES + jnp.bitwise_xor(core, other)
            for index, offset in enumerate(near):
                owner = lax.rem(z + offset + Z, Z)
                for slot in range(2):
                    wanted = jnp.bitwise_and(request_ref[row, owner * 2 + slot], count - 1)
                    value = block(index, wanted)
                    if shift:
                        send_refs[shift - 1][other, index, slot] = value
                    elif other:
                        core_ref[index, slot] = value
                    else:
                        own_ref[index, slot] = value


def make_pick(near, count, request, place, sources):
    piece = sources[0].shape[1:]
    one = jax.ShapeDtypeStruct((len(near), 2) + piece, jnp.bfloat16)
    both = jax.ShapeDtypeStruct((CORES, len(near), 2) + piece, jnp.bfloat16)
    return pl.pallas_call(
        functools.partial(pick_kernel, near, count),
        out_shape=(one, one) + (both,) * (Y - 1),
        in_specs=[SMEM, SMEM] + [VMEM] * len(sources),
        out_specs=(VMEM,) * (1 + Y),
        compiler_params=pltpu.CompilerParams(vmem_limit_bytes=VMEM_LIMIT),
        name="pick_blocks",
    )(request, place, *sources)


def sum_kernel(where_ref, tiles_ref, bias_ref, *refs):
    *parts, out_ref, got_ref = refs
    start = 0
    for chunk in range(0, len(parts), Y + 1):
        own_ref, *arrived, swapped_ref = parts[chunk : chunk + Y + 1]
        pairs = own_ref.shape[0]
        for shift in range(Y):
            for other in range(CORES):
                base = (shift * CORES + other) * Z * 2 + start
                for pair in range(pairs):
                    for slot in range(2):
                        if other:
                            value = swapped_ref[shift, pair, slot]
                        elif shift:
                            value = arrived[shift - 1][0, pair, slot]
                        else:
                            value = own_ref[pair, slot]
                        got_ref[base + pair * 2 + slot] = value
        start += pairs * 2
    rows, slots, size, _ = tiles_ref.shape
    for row in range(rows):
        pieces = [got_ref[where_ref[row * slots + slot]] for slot in range(slots)]
        gathered = jnp.concatenate(pieces, axis=1)
        tiles = jnp.concatenate([tiles_ref[row, slot] for slot in range(slots)], axis=1)
        summed = lax.dot_general(
            gathered, tiles, (((1,), (1,)), ((), ())), preferred_element_type=jnp.float32
        )
        out_ref[:, row * size : (row + 1) * size] = jnp.maximum(
            summed + bias_ref[...], 0.0
        ).astype(out_ref.dtype)


def make_sum(where, tiles, bias, parts):
    rows, slots, size, _ = tiles.shape
    width = bias.shape[0]
    return pl.pallas_call(
        sum_kernel,
        out_shape=jax.ShapeDtypeStruct((width, rows * size), jnp.bfloat16),
        in_specs=[SMEM, VMEM, VMEM] + [VMEM] * len(parts),
        out_specs=VMEM,
        scratch_shapes=[pltpu.VMEM((rows * slots, width, size), jnp.bfloat16)],
        compiler_params=pltpu.CompilerParams(vmem_limit_bytes=VMEM_LIMIT),
        name="sum_tiles",
    )(where, tiles, bias, *parts)


def load_kernel(counts_ref, tiles_ref, used_ref):
    rows, slots = tiles_ref.shape[:2]

    def load(row, carry):
        for slot in range(slots):
            tile = tiles_ref[row, slot]
            used_ref[row, slot] = jnp.where(slot < counts_ref[row], tile, jnp.zeros_like(tile))
        return carry

    lax.fori_loop(0, rows, load, 0, unroll=2)


def make_load(counts, tiles):
    return pl.pallas_call(
        load_kernel,
        out_shape=jax.ShapeDtypeStruct(tiles.shape, tiles.dtype),
        in_specs=[SMEM, VMEM],
        out_specs=VMEM,
        compiler_params=pltpu.CompilerParams(vmem_limit_bytes=VMEM_LIMIT),
        cost_estimate=pl.CostEstimate(flops=0, bytes_accessed=8_000_000, transcendentals=0),
        name="load_tiles",
    )(counts, tiles)


def dom_index(y, z, core):
    return (y * Z + z) * CORES + core


def move(array, shift_y, shift_z, other):
    pairs = [
        (
            dom_index(y, z, core),
            dom_index((y + shift_y) % Y, (z + shift_z) % Z, core ^ other),
        )
        for y in range(Y)
        for z in range(Z)
        for core in range(CORES)
    ]
    return lax.ppermute(array, "dom", pairs)


def body(features, order, weight, bias, tiles, col_ids, counts):
    nodes, width = features.shape
    rows, slots, size, _ = tiles.shape
    reps = lax.axis_size("rep")
    rep = lax.axis_index("rep").astype(jnp.int32)
    dom = lax.axis_index("dom").astype(jnp.int32)
    y, z, core = dom // (Z * CORES), (dom // CORES) % Z, dom % CORES
    mine = jnp.concatenate([features.T, weight], axis=1)
    parts = [mine] + [
        lax.ppermute(mine, "rep", [(i, (i + shift) % reps) for i in range(reps)])
        for shift in range(1, reps)
    ]

    ids = col_ids.reshape(-1)
    total = ids.shape[0]
    owner = ids // rows
    slot = jnp.arange(total, dtype=jnp.int32)
    code = slot * rows + ids % rows
    row = lax.broadcasted_iota(jnp.int32, (Y * CORES, 128), 0)
    lane = lax.broadcasted_iota(jnp.int32, (Y * CORES, 128), 1)
    asked = dom_index(row // CORES, (lane // 2) % Z, row % CORES)
    match = owner[None, None, :] == asked[:, :, None]
    first = jnp.min(jnp.where(match, code[None, None, :], total * rows), axis=2)
    last = jnp.max(jnp.where(match, code[None, None, :], -1), axis=2)
    request = jnp.where(lane % 2 == 0, first, last) % rows
    groups = [
        [dom_index(group_y, group_z, group_core) for group_y in range(Y) for group_core in range(CORES)]
        for group_z in range(Z)
    ]
    request = lax.all_to_all(request, "dom", 0, 0, axis_index_groups=groups, tiled=True)

    earlier = (owner[None, :] == owner[:, None]) & (slot[None, :] < slot[:, None])
    rank = jnp.any(earlier, axis=1).astype(jnp.int32)
    away = ((owner // CORES) % Z - z) % Z
    found = jnp.zeros_like(away)
    for index, offset in enumerate(sum(CHUNKS, ())):
        found = jnp.where(away == offset % Z, index, found)
    shift = (y - owner // (Z * CORES)) % Y
    other = jnp.bitwise_xor(owner % CORES, core)
    where = ((shift * CORES + other) * Z + found) * 2 + rank

    order = jnp.bitwise_and(order, nodes - 1)
    request, order, *parts = lax.optimization_barrier((request, order, *parts))
    blocks = make_hidden(rep[None], order, parts, width, nodes, size)
    ups, downs = [blocks, move(blocks, 0, 1, 0)], [blocks, move(blocks, 0, -1, 0)]
    used = make_load(counts, tiles)
    ups[1], downs[1], used = lax.optimization_barrier((ups[1], downs[1], used))
    for _ in range(Z // 2 - 2):
        ups.append(move(ups[-1], 0, 1, 0))
        downs.append(move(downs[-1], 0, -1, 0))
    half = rows // 2
    opposite = [move(ups[-1][:half], 0, 1, 0), move(downs[-1][half:], 0, -1, 0)]
    held = {0: [blocks], -Z // 2: opposite}
    for step in range(1, Z // 2):
        held[-step] = [ups[step]]
        held[step] = [downs[step]]
    held[Z // 2] = opposite

    place = jnp.stack([y, z, core])
    got = []
    for near in CHUNKS:
        sources = [array for offset in near for array in held[offset]]
        own, swap, *sends = make_pick(near, rows, request, place, sources)
        arrived = [move(send, step + 1, 0, 0) for step, send in enumerate(sends)]
        swap = jnp.stack([swap] + [array[1] for array in arrived])
        got += [own] + arrived + [move(swap, 0, 0, 1)]
    return make_sum(where, used, bias[:, None], got).T


def solution(mesh):
    in_specs = (
        P("dom", "rep"),
        P("dom", None),
        P("rep", None),
        P("rep"),
        P("dom", None, None, None),
        P("dom", None),
        P("dom"),
    )
    out_specs = P("dom", "rep")
    return jax.shard_map(body, mesh=mesh, in_specs=in_specs, out_specs=out_specs, check_vma=False)
```

```python
import functools

import jax
import jax.numpy as jnp
from jax import lax
from jax.experimental import pallas as pl
from jax.experimental.pallas import tpu as pltpu
from jax.sharding import PartitionSpec as P

VMEM_LIMIT = 24 * 1024 * 1024
VMEM = pl.BlockSpec(memory_space=pltpu.VMEM)
SMEM = pl.BlockSpec(memory_space=pltpu.SMEM)
Y, Z, CORES = 4, 8, 2
CHUNKS = ((0, -1), (1, -2, 2), (-3, 3), (4,))


def hidden_kernel(rep_ref, order_ref, x0_ref, x1_ref, x2_ref, x3_ref, blocks_ref):
    width = x0_ref.shape[0]
    count, _, size = blocks_ref.shape
    nodes = count * size
    rep = rep_ref[0]
    weights = []
    features = []
    for part in (x0_ref, x1_ref, x2_ref, x3_ref):
        columns = part[:, nodes : nodes + width]
        for index in range(1, (part.shape[1] - nodes) // width):
            other = part[:, nodes + index * width : nodes + (index + 1) * width]
            columns = jnp.where(rep == index, other, columns)
        weights.append(columns)
        features.append(part[:, :nodes])
    total = lax.dot_general(
        jnp.concatenate(weights, axis=0),
        jnp.concatenate(features, axis=0),
        (((0,), (0,)), ((), ())),
        preferred_element_type=jnp.float32,
    )
    hidden = total.astype(jnp.bfloat16).astype(jnp.float32)
    for block in range(count):
        order = order_ref[:, block * size : (block + 1) * size]
        order = jnp.broadcast_to(order, (width, size))
        lane = jnp.bitwise_and(order, size - 1)
        chunk = lax.shift_right_logical(order, size.bit_length() - 1)
        value = jnp.zeros((width, size), jnp.float32)
        for source in range(count):
            piece = hidden[:, source * size : (source + 1) * size]
            picked = jnp.take_along_axis(piece, lane, axis=1)
            value = jnp.where(chunk == source, picked, value)
        blocks_ref[block] = value.astype(jnp.bfloat16)


def make_hidden(rep, order, parts, width, nodes, size):
    return pl.pallas_call(
        hidden_kernel,
        out_shape=jax.ShapeDtypeStruct((nodes // size, width, size), jnp.bfloat16),
        in_specs=[SMEM] + [VMEM] * (1 + len(parts)),
        out_specs=VMEM,
        compiler_params=pltpu.CompilerParams(vmem_limit_bytes=VMEM_LIMIT),
        cost_estimate=pl.CostEstimate(flops=400_000_000, bytes_accessed=8_000_000, transcendentals=0),
        name="hidden_blocks",
    )(rep, order, *parts)


def pick_kernel(near, count, request_ref, place_ref, *refs):
    own_ref, core_ref, *send_refs = refs[-(1 + Y) :]
    sources = refs[: -(1 + Y)]
    y, z, core = place_ref[0], place_ref[1], place_ref[2]
    half = count // 2

    def block(index, wanted):
        if index < len(near) - 1 or near[index] != Z // 2:
            return sources[index][wanted]
        low = sources[index][jnp.minimum(wanted, half - 1)]
        high = sources[index + 1][jnp.maximum(wanted - half, 0)]
        return jnp.where(wanted < half, low, high)

    for shift in range(Y):
        for other in range(CORES):
            row = lax.rem(y + shift, Y) * CORES + jnp.bitwise_xor(core, other)
            for index, offset in enumerate(near):
                owner = lax.rem(z + offset * (1 - jnp.bitwise_and(z, 1) * 2) + Z, Z)
                for slot in range(2):
                    wanted = jnp.bitwise_and(request_ref[row, owner * 2 + slot], count - 1)
                    value = block(index, wanted)
                    if shift:
                        send_refs[shift - 1][other, index, slot] = value
                    elif other:
                        core_ref[index, slot] = value
                    else:
                        own_ref[index, slot] = value


def make_pick(near, count, request, place, sources):
    piece = sources[0].shape[1:]
    one = jax.ShapeDtypeStruct((len(near), 2) + piece, jnp.bfloat16)
    both = jax.ShapeDtypeStruct((CORES, len(near), 2) + piece, jnp.bfloat16)
    return pl.pallas_call(
        functools.partial(pick_kernel, near, count),
        out_shape=(one, one) + (both,) * (Y - 1),
        in_specs=[SMEM, SMEM] + [VMEM] * len(sources),
        out_specs=(VMEM,) * (1 + Y),
        compiler_params=pltpu.CompilerParams(vmem_limit_bytes=VMEM_LIMIT),
        name="pick_blocks",
    )(request, place, *sources)


def sum_kernel(where_ref, tiles_ref, bias_ref, *refs):
    *parts, out_ref, got_ref = refs
    start = 0
    for chunk in range(0, len(parts), Y + 1):
        own_ref, *arrived, swapped_ref = parts[chunk : chunk + Y + 1]
        pairs = own_ref.shape[0]
        for shift in range(Y):
            for other in range(CORES):
                base = (shift * CORES + other) * Z * 2 + start
                for pair in range(pairs):
                    for slot in range(2):
                        if other:
                            value = swapped_ref[shift, pair, slot]
                        elif shift:
                            value = arrived[shift - 1][0, pair, slot]
                        else:
                            value = own_ref[pair, slot]
                        got_ref[base + pair * 2 + slot] = value
        start += pairs * 2
    rows, slots, size, _ = tiles_ref.shape
    for row in range(rows):
        pieces = [got_ref[where_ref[row * slots + slot]] for slot in range(slots)]
        gathered = jnp.concatenate(pieces, axis=1)
        tiles = jnp.concatenate([tiles_ref[row, slot] for slot in range(slots)], axis=1)
        summed = lax.dot_general(
            gathered, tiles, (((1,), (1,)), ((), ())), preferred_element_type=jnp.float32
        )
        out_ref[:, row * size : (row + 1) * size] = jnp.maximum(
            summed + bias_ref[...], 0.0
        ).astype(out_ref.dtype)


def make_sum(where, tiles, bias, parts):
    rows, slots, size, _ = tiles.shape
    width = bias.shape[0]
    return pl.pallas_call(
        sum_kernel,
        out_shape=jax.ShapeDtypeStruct((width, rows * size), jnp.bfloat16),
        in_specs=[SMEM, VMEM, VMEM] + [VMEM] * len(parts),
        out_specs=VMEM,
        scratch_shapes=[pltpu.VMEM((rows * slots, width, size), jnp.bfloat16)],
        compiler_params=pltpu.CompilerParams(vmem_limit_bytes=VMEM_LIMIT),
        name="sum_tiles",
    )(where, tiles, bias, *parts)


def load_kernel(counts_ref, tiles_ref, used_ref):
    rows, slots = tiles_ref.shape[:2]

    def load(row, carry):
        for slot in range(slots):
            tile = tiles_ref[row, slot]
            used_ref[row, slot] = jnp.where(slot < counts_ref[row], tile, jnp.zeros_like(tile))
        return carry

    lax.fori_loop(0, rows, load, 0, unroll=2)


def make_load(counts, tiles):
    return pl.pallas_call(
        load_kernel,
        out_shape=jax.ShapeDtypeStruct(tiles.shape, tiles.dtype),
        in_specs=[SMEM, VMEM],
        out_specs=VMEM,
        compiler_params=pltpu.CompilerParams(vmem_limit_bytes=VMEM_LIMIT),
        cost_estimate=pl.CostEstimate(flops=0, bytes_accessed=8_000_000, transcendentals=0),
        name="load_tiles",
    )(counts, tiles)


def dom_index(y, z, core):
    return (y * Z + z) * CORES + core


def move(array, shift_y, side, other):
    pairs = [
        (
            dom_index(y, z, core),
            dom_index((y + shift_y) % Y, (z + side * (1 - z % 2 * 2)) % Z, core ^ other),
        )
        for y in range(Y)
        for z in range(Z)
        for core in range(CORES)
    ]
    return lax.ppermute(array, "dom", pairs)


def body(features, order, weight, bias, tiles, col_ids, counts):
    nodes, width = features.shape
    rows, slots, size, _ = tiles.shape
    reps = lax.axis_size("rep")
    rep = lax.axis_index("rep").astype(jnp.int32)
    dom = lax.axis_index("dom").astype(jnp.int32)
    y, z, core = dom // (Z * CORES), (dom // CORES) % Z, dom % CORES
    mine = jnp.concatenate([features.T, weight], axis=1)
    parts = [mine] + [
        lax.ppermute(mine, "rep", [(i, (i + shift) % reps) for i in range(reps)])
        for shift in range(1, reps)
    ]

    ids = col_ids.reshape(-1)
    total = ids.shape[0]
    owner = ids // rows
    slot = jnp.arange(total, dtype=jnp.int32)
    code = slot * rows + ids % rows
    row = lax.broadcasted_iota(jnp.int32, (Y * CORES, 128), 0)
    lane = lax.broadcasted_iota(jnp.int32, (Y * CORES, 128), 1)
    asked = dom_index(row // CORES, (lane // 2) % Z, row % CORES)
    match = owner[None, None, :] == asked[:, :, None]
    first = jnp.min(jnp.where(match, code[None, None, :], total * rows), axis=2)
    last = jnp.max(jnp.where(match, code[None, None, :], -1), axis=2)
    request = jnp.where(lane % 2 == 0, first, last) % rows
    groups = [
        [dom_index(group_y, group_z, group_core) for group_y in range(Y) for group_core in range(CORES)]
        for group_z in range(Z)
    ]
    request = lax.all_to_all(request, "dom", 0, 0, axis_index_groups=groups, tiled=True)

    earlier = (owner[None, :] == owner[:, None]) & (slot[None, :] < slot[:, None])
    rank = jnp.any(earlier, axis=1).astype(jnp.int32)
    away = ((owner // CORES) % Z - z) * (1 - z % 2 * 2) % Z
    found = jnp.zeros_like(away)
    for index, offset in enumerate(sum(CHUNKS, ())):
        found = jnp.where(away == offset % Z, index, found)
    shift = (y - owner // (Z * CORES)) % Y
    other = jnp.bitwise_xor(owner % CORES, core)
    where = ((shift * CORES + other) * Z + found) * 2 + rank

    order = jnp.bitwise_and(order, nodes - 1)
    request, order, *parts = lax.optimization_barrier((request, order, *parts))
    blocks = make_hidden(rep[None], order, parts, width, nodes, size)
    ups, downs = [blocks, move(blocks, 0, 1, 0)], [blocks, move(blocks, 0, -1, 0)]
    used = make_load(counts, tiles)
    ups[1], downs[1], used = lax.optimization_barrier((ups[1], downs[1], used))
    for _ in range(Z // 2 - 2):
        after, before = move(downs[-1], 0, 1, 0), move(ups[-1], 0, -1, 0)
        ups.append(after)
        downs.append(before)
    half = rows // 2
    opposite = [move(downs[-1][:half], 0, 1, 0), move(ups[-1][half:], 0, -1, 0)]
    held = {0: [blocks], -Z // 2: opposite}
    for step in range(1, Z // 2):
        held[step] = [ups[step]]
        held[-step] = [downs[step]]
    held[Z // 2] = opposite

    place = jnp.stack([y, z, core])
    got = []
    for near in CHUNKS:
        sources = [array for offset in near for array in held[offset]]
        own, swap, *sends = make_pick(near, rows, request, place, sources)
        arrived = [move(send, step + 1, 0, 0) for step, send in enumerate(sends)]
        swap = jnp.stack([swap] + [array[1] for array in arrived])
        got += [own] + arrived + [move(swap, 0, 0, 1)]
    return make_sum(where, used, bias[:, None], got).T


def solution(mesh):
    in_specs = (
        P("dom", "rep"),
        P("dom", None),
        P("rep", None),
        P("rep"),
        P("dom", None, None, None),
        P("dom", None),
        P("dom"),
    )
    out_specs = P("dom", "rep")
    return jax.shard_map(body, mesh=mesh, in_specs=in_specs, out_specs=out_specs, check_vma=False)
```

```python
import functools

import jax
import jax.numpy as jnp
from jax import lax
from jax.experimental import pallas as pl
from jax.experimental.pallas import tpu as pltpu
from jax.sharding import PartitionSpec as P

VMEM_LIMIT = 24 * 1024 * 1024
LOAD_STEPS = 4
VMEM = pl.BlockSpec(memory_space=pltpu.VMEM)
SMEM = pl.BlockSpec(memory_space=pltpu.SMEM)
Y, Z, CORES = 4, 8, 2
CHUNKS = ((0, -1), (1, -2, 2), (-3, 3), (4,))


def hidden_kernel(rep_ref, order_ref, x0_ref, x1_ref, x2_ref, x3_ref, blocks_ref):
    width = x0_ref.shape[0]
    count, _, size = blocks_ref.shape
    nodes = count * size
    rep = rep_ref[0]
    weights = []
    features = []
    for part in (x0_ref, x1_ref, x2_ref, x3_ref):
        columns = part[:, nodes : nodes + width]
        for index in range(1, (part.shape[1] - nodes) // width):
            other = part[:, nodes + index * width : nodes + (index + 1) * width]
            columns = jnp.where(rep == index, other, columns)
        weights.append(columns)
        features.append(part[:, :nodes])
    total = lax.dot_general(
        jnp.concatenate(weights, axis=0),
        jnp.concatenate(features, axis=0),
        (((0,), (0,)), ((), ())),
        preferred_element_type=jnp.float32,
    )
    hidden = total.astype(jnp.bfloat16).astype(jnp.float32)
    for block in range(count):
        order = order_ref[:, block * size : (block + 1) * size]
        order = jnp.broadcast_to(order, (width, size))
        lane = jnp.bitwise_and(order, size - 1)
        chunk = lax.shift_right_logical(order, size.bit_length() - 1)
        value = jnp.zeros((width, size), jnp.float32)
        for source in range(count):
            piece = hidden[:, source * size : (source + 1) * size]
            picked = jnp.take_along_axis(piece, lane, axis=1)
            value = jnp.where(chunk == source, picked, value)
        blocks_ref[block] = value.astype(jnp.bfloat16)


def make_hidden(rep, order, parts, width, nodes, size):
    return pl.pallas_call(
        hidden_kernel,
        out_shape=jax.ShapeDtypeStruct((nodes // size, width, size), jnp.bfloat16),
        in_specs=[SMEM] + [VMEM] * (1 + len(parts)),
        out_specs=VMEM,
        compiler_params=pltpu.CompilerParams(vmem_limit_bytes=VMEM_LIMIT),
        cost_estimate=pl.CostEstimate(flops=400_000_000, bytes_accessed=8_000_000, transcendentals=0),
        name="hidden_blocks",
    )(rep, order, *parts)


def pick_kernel(near, count, request_ref, place_ref, *refs):
    own_ref, core_ref, *send_refs = refs[-(1 + Y) :]
    sources = refs[: -(1 + Y)]
    y, z, core = place_ref[0], place_ref[1], place_ref[2]
    half = count // 2

    def block(index, wanted):
        if index < len(near) - 1 or near[index] != Z // 2:
            return sources[index][wanted]
        low = sources[index][jnp.minimum(wanted, half - 1)]
        high = sources[index + 1][jnp.maximum(wanted - half, 0)]
        return jnp.where(wanted < half, low, high)

    for shift in range(Y):
        for other in range(CORES):
            row = lax.rem(y + shift, Y) * CORES + jnp.bitwise_xor(core, other)
            for index, offset in enumerate(near):
                owner = lax.rem(z + offset * (1 - jnp.bitwise_and(z, 1) * 2) + Z, Z)
                for slot in range(2):
                    wanted = jnp.bitwise_and(request_ref[row, owner * 2 + slot], count - 1)
                    value = block(index, wanted)
                    if shift:
                        send_refs[shift - 1][other, index, slot] = value
                    elif other:
                        core_ref[index, slot] = value
                    else:
                        own_ref[index, slot] = value


def make_pick(near, count, request, place, sources):
    piece = sources[0].shape[1:]
    one = jax.ShapeDtypeStruct((len(near), 2) + piece, jnp.bfloat16)
    both = jax.ShapeDtypeStruct((CORES, len(near), 2) + piece, jnp.bfloat16)
    return pl.pallas_call(
        functools.partial(pick_kernel, near, count),
        out_shape=(one, one) + (both,) * (Y - 1),
        in_specs=[SMEM, SMEM] + [VMEM] * len(sources),
        out_specs=(VMEM,) * (1 + Y),
        compiler_params=pltpu.CompilerParams(vmem_limit_bytes=VMEM_LIMIT),
        name="pick_blocks",
    )(request, place, *sources)


def sum_kernel(where_ref, tiles_ref, bias_ref, *refs):
    *parts, out_ref, got_ref = refs
    start = 0
    for chunk in range(0, len(parts), Y + 1):
        own_ref, *arrived, swapped_ref = parts[chunk : chunk + Y + 1]
        pairs = own_ref.shape[0]
        for shift in range(Y):
            for other in range(CORES):
                base = (shift * CORES + other) * Z * 2 + start
                for pair in range(pairs):
                    for slot in range(2):
                        if other:
                            value = swapped_ref[shift, pair, slot]
                        elif shift:
                            value = arrived[shift - 1][0, pair, slot]
                        else:
                            value = own_ref[pair, slot]
                        got_ref[base + pair * 2 + slot] = value
        start += pairs * 2
    rows, slots, size, _ = tiles_ref.shape
    for row in range(rows):
        pieces = [got_ref[where_ref[row * slots + slot]] for slot in range(slots)]
        gathered = jnp.concatenate(pieces, axis=1)
        tiles = jnp.concatenate([tiles_ref[row, slot] for slot in range(slots)], axis=1)
        summed = lax.dot_general(
            gathered, tiles, (((1,), (1,)), ((), ())), preferred_element_type=jnp.float32
        )
        out_ref[:, row * size : (row + 1) * size] = jnp.maximum(
            summed + bias_ref[...], 0.0
        ).astype(out_ref.dtype)


def make_sum(where, tiles, bias, parts):
    rows, slots, size, _ = tiles.shape
    width = bias.shape[0]
    return pl.pallas_call(
        sum_kernel,
        out_shape=jax.ShapeDtypeStruct((width, rows * size), jnp.bfloat16),
        in_specs=[SMEM, VMEM, VMEM] + [VMEM] * len(parts),
        out_specs=VMEM,
        scratch_shapes=[pltpu.VMEM((rows * slots, width, size), jnp.bfloat16)],
        compiler_params=pltpu.CompilerParams(vmem_limit_bytes=VMEM_LIMIT),
        name="sum_tiles",
    )(where, tiles, bias, *parts)


def load_kernel(counts_ref, tiles_ref, used_ref):
    rows, slots = tiles_ref.shape[:2]
    first = pl.program_id(0) * rows
    for row in range(rows):
        used = counts_ref[first + row]
        for slot in range(slots):
            tile = tiles_ref[row, slot]
            used_ref[row, slot] = jnp.where(slot < used, tile, jnp.zeros_like(tile))


def make_load(counts, tiles):
    rows = tiles.shape[0] // LOAD_STEPS
    block = pl.BlockSpec((rows,) + tiles.shape[1:], lambda index: (index, 0, 0, 0))
    return pl.pallas_call(
        load_kernel,
        grid=(LOAD_STEPS,),
        out_shape=jax.ShapeDtypeStruct(tiles.shape, tiles.dtype),
        in_specs=[SMEM, block],
        out_specs=block,
        compiler_params=pltpu.CompilerParams(vmem_limit_bytes=VMEM_LIMIT),
        cost_estimate=pl.CostEstimate(flops=0, bytes_accessed=8_000_000, transcendentals=0),
        name="load_tiles",
    )(counts, tiles)


def dom_index(y, z, core):
    return (y * Z + z) * CORES + core


def move(array, shift_y, side, other):
    pairs = [
        (
            dom_index(y, z, core),
            dom_index((y + shift_y) % Y, (z + side * (1 - z % 2 * 2)) % Z, core ^ other),
        )
        for y in range(Y)
        for z in range(Z)
        for core in range(CORES)
    ]
    return lax.ppermute(array, "dom", pairs)


def body(features, order, weight, bias, tiles, col_ids, counts):
    nodes, width = features.shape
    rows, slots, size, _ = tiles.shape
    reps = lax.axis_size("rep")
    rep = lax.axis_index("rep").astype(jnp.int32)
    dom = lax.axis_index("dom").astype(jnp.int32)
    y, z, core = dom // (Z * CORES), (dom // CORES) % Z, dom % CORES
    mine = jnp.concatenate([features.T, weight], axis=1)
    parts = [mine] + [
        lax.ppermute(mine, "rep", [(i, (i + shift) % reps) for i in range(reps)])
        for shift in range(1, reps)
    ]

    ids = col_ids.reshape(-1)
    total = ids.shape[0]
    owner = ids // rows
    slot = jnp.arange(total, dtype=jnp.int32)
    code = slot * rows + ids % rows
    row = lax.broadcasted_iota(jnp.int32, (Y * CORES, 128), 0)
    lane = lax.broadcasted_iota(jnp.int32, (Y * CORES, 128), 1)
    asked = dom_index(row // CORES, (lane // 2) % Z, row % CORES)
    match = owner[None, None, :] == asked[:, :, None]
    first = jnp.min(jnp.where(match, code[None, None, :], total * rows), axis=2)
    last = jnp.max(jnp.where(match, code[None, None, :], -1), axis=2)
    request = jnp.where(lane % 2 == 0, first, last) % rows
    groups = [
        [dom_index(group_y, group_z, group_core) for group_y in range(Y) for group_core in range(CORES)]
        for group_z in range(Z)
    ]
    request = lax.all_to_all(request, "dom", 0, 0, axis_index_groups=groups, tiled=True)

    earlier = (owner[None, :] == owner[:, None]) & (slot[None, :] < slot[:, None])
    rank = jnp.any(earlier, axis=1).astype(jnp.int32)
    away = ((owner // CORES) % Z - z) * (1 - z % 2 * 2) % Z
    found = jnp.zeros_like(away)
    for index, offset in enumerate(sum(CHUNKS, ())):
        found = jnp.where(away == offset % Z, index, found)
    shift = (y - owner // (Z * CORES)) % Y
    other = jnp.bitwise_xor(owner % CORES, core)
    where = ((shift * CORES + other) * Z + found) * 2 + rank

    order = jnp.bitwise_and(order, nodes - 1)
    request, order, *parts = lax.optimization_barrier((request, order, *parts))
    blocks = make_hidden(rep[None], order, parts, width, nodes, size)
    ups, downs = [blocks, move(blocks, 0, 1, 0)], [blocks, move(blocks, 0, -1, 0)]
    used = make_load(counts, tiles)
    ups[1], downs[1], used = lax.optimization_barrier((ups[1], downs[1], used))
    for _ in range(Z // 2 - 2):
        after, before = move(downs[-1], 0, 1, 0), move(ups[-1], 0, -1, 0)
        ups.append(after)
        downs.append(before)
    half = rows // 2
    opposite = [move(downs[-1][:half], 0, 1, 0), move(ups[-1][half:], 0, -1, 0)]
    held = {0: [blocks], -Z // 2: opposite}
    for step in range(1, Z // 2):
        held[step] = [ups[step]]
        held[-step] = [downs[step]]
    held[Z // 2] = opposite

    place = jnp.stack([y, z, core])
    got = []
    for near in CHUNKS:
        sources = [array for offset in near for array in held[offset]]
        own, swap, *sends = make_pick(near, rows, request, place, sources)
        arrived = [move(send, step + 1, 0, 0) for step, send in enumerate(sends)]
        swap = jnp.stack([swap] + [array[1] for array in arrived])
        got += [own] + arrived + [move(swap, 0, 0, 1)]
    return make_sum(where, used, bias[:, None], got).T


def solution(mesh):
    in_specs = (
        P("dom", "rep"),
        P("dom", None),
        P("rep", None),
        P("rep"),
        P("dom", None, None, None),
        P("dom", None),
        P("dom"),
    )
    out_specs = P("dom", "rep")
    return jax.shard_map(body, mesh=mesh, in_specs=in_specs, out_specs=out_specs, check_vma=False)
```

```python
import functools

import jax
import jax.numpy as jnp
from jax import lax
from jax.experimental import pallas as pl
from jax.experimental.pallas import tpu as pltpu
from jax.sharding import PartitionSpec as P

VMEM_LIMIT = 24 * 1024 * 1024
LOAD_STEPS = 4
VMEM = pl.BlockSpec(memory_space=pltpu.VMEM)
SMEM = pl.BlockSpec(memory_space=pltpu.SMEM)
Y, Z, CORES = 4, 8, 2
CHUNKS = ((0, -1), (1, -2, 2), (-3, 3), (4,))


def hidden_kernel(rep_ref, order_ref, x0_ref, x1_ref, x2_ref, x3_ref, blocks_ref):
    width = x0_ref.shape[0]
    count, _, size = blocks_ref.shape
    nodes = count * size
    rep = rep_ref[0]
    weights = []
    features = []
    for part in (x0_ref, x1_ref, x2_ref, x3_ref):
        columns = part[:, nodes : nodes + width]
        for index in range(1, (part.shape[1] - nodes) // width):
            other = part[:, nodes + index * width : nodes + (index + 1) * width]
            columns = jnp.where(rep == index, other, columns)
        weights.append(columns)
        features.append(part[:, :nodes])
    total = lax.dot_general(
        jnp.concatenate(weights, axis=0),
        jnp.concatenate(features, axis=0),
        (((0,), (0,)), ((), ())),
        preferred_element_type=jnp.float32,
    )
    hidden = total.astype(jnp.bfloat16).astype(jnp.float32)
    for block in range(count):
        order = order_ref[:, block * size : (block + 1) * size]
        order = jnp.broadcast_to(order, (width, size))
        lane = jnp.bitwise_and(order, size - 1)
        chunk = lax.shift_right_logical(order, size.bit_length() - 1)
        value = jnp.zeros((width, size), jnp.float32)
        for source in range(count):
            piece = hidden[:, source * size : (source + 1) * size]
            picked = jnp.take_along_axis(piece, lane, axis=1)
            value = jnp.where(chunk == source, picked, value)
        blocks_ref[block] = value.astype(jnp.bfloat16)


def make_hidden(rep, order, parts, width, nodes, size):
    return pl.pallas_call(
        hidden_kernel,
        out_shape=jax.ShapeDtypeStruct((nodes // size, width, size), jnp.bfloat16),
        in_specs=[SMEM] + [VMEM] * (1 + len(parts)),
        out_specs=VMEM,
        compiler_params=pltpu.CompilerParams(vmem_limit_bytes=VMEM_LIMIT),
        cost_estimate=pl.CostEstimate(flops=400_000_000, bytes_accessed=8_000_000, transcendentals=0),
        name="hidden_blocks",
    )(rep, order, *parts)


def pick_kernel(near, count, request_ref, place_ref, *refs):
    own_ref, core_ref, *send_refs = refs[-(1 + Y) :]
    sources = refs[: -(1 + Y)]
    y, z, core = place_ref[0], place_ref[1], place_ref[2]
    half = count // 2

    def block(index, wanted):
        if index < len(near) - 1 or near[index] != Z // 2:
            return sources[index][wanted]
        low = sources[index][jnp.minimum(wanted, half - 1)]
        high = sources[index + 1][jnp.maximum(wanted - half, 0)]
        return jnp.where(wanted < half, low, high)

    for shift in range(Y):
        for other in range(CORES):
            row = lax.rem(y + shift, Y) * CORES + jnp.bitwise_xor(core, other)
            for index, offset in enumerate(near):
                owner = lax.rem(z + offset * (1 - jnp.bitwise_and(z, 1) * 2) + Z, Z)
                for slot in range(2):
                    wanted = jnp.bitwise_and(request_ref[row, owner * 2 + slot], count - 1)
                    value = block(index, wanted)
                    if shift:
                        send_refs[shift - 1][other, index, slot] = value
                    elif other:
                        core_ref[index, slot] = value
                    else:
                        own_ref[index, slot] = value


def make_pick(near, count, request, place, sources):
    piece = sources[0].shape[1:]
    one = jax.ShapeDtypeStruct((len(near), 2) + piece, jnp.bfloat16)
    both = jax.ShapeDtypeStruct((CORES, len(near), 2) + piece, jnp.bfloat16)
    return pl.pallas_call(
        functools.partial(pick_kernel, near, count),
        out_shape=(one, one) + (both,) * (Y - 1),
        in_specs=[SMEM, SMEM] + [VMEM] * len(sources),
        out_specs=(VMEM,) * (1 + Y),
        compiler_params=pltpu.CompilerParams(vmem_limit_bytes=VMEM_LIMIT),
        name="pick_blocks",
    )(request, place, *sources)


def sum_kernel(where_ref, tiles_ref, bias_ref, *refs):
    *parts, out_ref, got_ref = refs
    start = 0
    for chunk in range(0, len(parts), Y + 1):
        own_ref, *arrived, swapped_ref = parts[chunk : chunk + Y + 1]
        pairs = own_ref.shape[0]
        for shift in range(Y):
            for other in range(CORES):
                base = (shift * CORES + other) * Z * 2 + start
                for pair in range(pairs):
                    for slot in range(2):
                        if other:
                            value = swapped_ref[shift, pair, slot]
                        elif shift:
                            value = arrived[shift - 1][0, pair, slot]
                        else:
                            value = own_ref[pair, slot]
                        got_ref[base + pair * 2 + slot] = value
        start += pairs * 2
    rows, slots, size, _ = tiles_ref.shape
    for row in range(rows):
        pieces = [got_ref[where_ref[row * slots + slot]] for slot in range(slots)]
        gathered = jnp.concatenate(pieces, axis=1)
        tiles = jnp.concatenate([tiles_ref[row, slot] for slot in range(slots)], axis=1)
        summed = lax.dot_general(
            gathered, tiles, (((1,), (1,)), ((), ())), preferred_element_type=jnp.float32
        )
        out_ref[:, row * size : (row + 1) * size] = jnp.maximum(
            summed + bias_ref[...], 0.0
        ).astype(out_ref.dtype)


def make_sum(where, tiles, bias, parts):
    rows, slots, size, _ = tiles.shape
    width = bias.shape[0]
    return pl.pallas_call(
        sum_kernel,
        out_shape=jax.ShapeDtypeStruct((width, rows * size), jnp.bfloat16),
        in_specs=[SMEM, VMEM, VMEM] + [VMEM] * len(parts),
        out_specs=VMEM,
        scratch_shapes=[pltpu.VMEM((rows * slots, width, size), jnp.bfloat16)],
        compiler_params=pltpu.CompilerParams(vmem_limit_bytes=VMEM_LIMIT),
        name="sum_tiles",
    )(where, tiles, bias, *parts)


def load_kernel(counts_ref, tiles_ref, used_ref):
    rows, slots = tiles_ref.shape[:2]
    first = pl.program_id(0) * rows
    for row in range(rows):
        used = counts_ref[first + row]
        for slot in range(slots):
            tile = tiles_ref[row, slot]
            used_ref[row, slot] = jnp.where(slot < used, tile, jnp.zeros_like(tile))


def make_load(counts, tiles):
    rows = tiles.shape[0] // LOAD_STEPS
    block = pl.BlockSpec((rows,) + tiles.shape[1:], lambda index: (index, 0, 0, 0))
    return pl.pallas_call(
        load_kernel,
        grid=(LOAD_STEPS,),
        out_shape=pltpu.HBM(tiles.shape, tiles.dtype),
        in_specs=[SMEM, block],
        out_specs=block,
        compiler_params=pltpu.CompilerParams(vmem_limit_bytes=VMEM_LIMIT),
        cost_estimate=pl.CostEstimate(flops=0, bytes_accessed=8_000_000, transcendentals=0),
        name="load_tiles",
    )(counts, tiles)


def dom_index(y, z, core):
    return (y * Z + z) * CORES + core


def move(array, shift_y, side, other):
    pairs = [
        (
            dom_index(y, z, core),
            dom_index((y + shift_y) % Y, (z + side * (1 - z % 2 * 2)) % Z, core ^ other),
        )
        for y in range(Y)
        for z in range(Z)
        for core in range(CORES)
    ]
    return lax.ppermute(array, "dom", pairs)


def body(features, order, weight, bias, tiles, col_ids, counts):
    nodes, width = features.shape
    rows, slots, size, _ = tiles.shape
    reps = lax.axis_size("rep")
    rep = lax.axis_index("rep").astype(jnp.int32)
    dom = lax.axis_index("dom").astype(jnp.int32)
    y, z, core = dom // (Z * CORES), (dom // CORES) % Z, dom % CORES
    mine = jnp.concatenate([features.T, weight], axis=1)
    parts = [mine] + [
        lax.ppermute(mine, "rep", [(i, (i + shift) % reps) for i in range(reps)])
        for shift in range(1, reps)
    ]

    ids = col_ids.reshape(-1)
    total = ids.shape[0]
    owner = ids // rows
    slot = jnp.arange(total, dtype=jnp.int32)
    code = slot * rows + ids % rows
    row = lax.broadcasted_iota(jnp.int32, (Y * CORES, 128), 0)
    lane = lax.broadcasted_iota(jnp.int32, (Y * CORES, 128), 1)
    asked = dom_index(row // CORES, (lane // 2) % Z, row % CORES)
    match = owner[None, None, :] == asked[:, :, None]
    first = jnp.min(jnp.where(match, code[None, None, :], total * rows), axis=2)
    last = jnp.max(jnp.where(match, code[None, None, :], -1), axis=2)
    request = jnp.where(lane % 2 == 0, first, last) % rows
    groups = [
        [dom_index(group_y, group_z, group_core) for group_y in range(Y) for group_core in range(CORES)]
        for group_z in range(Z)
    ]
    request = lax.all_to_all(request, "dom", 0, 0, axis_index_groups=groups, tiled=True)

    earlier = (owner[None, :] == owner[:, None]) & (slot[None, :] < slot[:, None])
    rank = jnp.any(earlier, axis=1).astype(jnp.int32)
    away = ((owner // CORES) % Z - z) * (1 - z % 2 * 2) % Z
    found = jnp.zeros_like(away)
    for index, offset in enumerate(sum(CHUNKS, ())):
        found = jnp.where(away == offset % Z, index, found)
    shift = (y - owner // (Z * CORES)) % Y
    other = jnp.bitwise_xor(owner % CORES, core)
    where = ((shift * CORES + other) * Z + found) * 2 + rank

    order = jnp.bitwise_and(order, nodes - 1)
    request, order, *parts = lax.optimization_barrier((request, order, *parts))
    blocks = make_hidden(rep[None], order, parts, width, nodes, size)
    ups, downs = [blocks, move(blocks, 0, 1, 0)], [blocks, move(blocks, 0, -1, 0)]
    used = make_load(counts, tiles)
    ups[1], downs[1], used = lax.optimization_barrier((ups[1], downs[1], used))
    for _ in range(Z // 2 - 2):
        after, before = move(downs[-1], 0, 1, 0), move(ups[-1], 0, -1, 0)
        ups.append(after)
        downs.append(before)
    half = rows // 2
    opposite = [move(downs[-1][:half], 0, 1, 0), move(ups[-1][half:], 0, -1, 0)]
    held = {0: [blocks], -Z // 2: opposite}
    for step in range(1, Z // 2):
        held[step] = [ups[step]]
        held[-step] = [downs[step]]
    held[Z // 2] = opposite

    place = jnp.stack([y, z, core])
    got = []
    for near in CHUNKS:
        sources = [array for offset in near for array in held[offset]]
        own, swap, *sends = make_pick(near, rows, request, place, sources)
        arrived = [move(send, step + 1, 0, 0) for step, send in enumerate(sends)]
        swap = jnp.stack([swap] + [array[1] for array in arrived])
        got += [own] + arrived + [move(swap, 0, 0, 1)]
    return make_sum(where, used, bias[:, None], got).T


def solution(mesh):
    in_specs = (
        P("dom", "rep"),
        P("dom", None),
        P("rep", None),
        P("rep"),
        P("dom", None, None, None),
        P("dom", None),
        P("dom"),
    )
    out_specs = P("dom", "rep")
    return jax.shard_map(body, mesh=mesh, in_specs=in_specs, out_specs=out_specs, check_vma=False)
```
